256 devices in a mesh: ev: 8 (over z), sp: 32 (over x, y, core).
Axes of the slice: x: 4, y: 4, z: 8, core: 2. Of those that a mesh axis runs over, the one named last changes fastest.
Arguments:
- kernels: bfloat16 [8, 3, 125, 32768], P('ev', None, None, 'sp'), may hold values from -6 to 6
- basis: bfloat16 [8, 125], replicated, may hold values from -0.5 to 0.5
- crossing: float32 [8, 4, 32768], P('ev', None, 'sp'), may hold values from 0.1 to 1
- owner: int32 [8, 4, 32768], P('ev', None, 'sp'), may hold values from 0 to 255, as said below
- target: int32 [8, 4, 32768], P('ev', None, 'sp'), may hold values from 0 to 8191
- diffusivity: float32 [32, 128, 512], P('ev', 'sp'), may hold values from 0.05 to 0.16
Outputs:
- smoothed: float32 [24, 32, 128, 512], P(None, 'ev', 'sp')
The draws below stay inside these ranges and needn't reach their ends.
Inputs may be any that keep to these rules, and one draw needn't show every extreme that they name: `owner`: event slabs and inversion blocks are geometrically aligned: the 4 x 1024 slots of the elements in slab j (elements j * 1024 to (j + 1) * 1024 - 1) of an event name only blocks of columns j - 1, j and j + 1 (block b lies in column b % 32); they name any one block at most 256 times, and every block of column j exactly 256 times.
All inputs are finite; a program needn't handle non-finite values.
Results may differ from the reference program's by a relative error of at most 0.0003.
Values sent between devices are 32-bit elements; how exact they have to be, the bound alone decides.
A program may use at most 128 MiB of HBM per device.

```python
import math
import jax
import jax.numpy as jnp
from jax import lax

PARAMS = 3
GLL = 125
NODES = 8
SLOTS = 4
STEPS = 4
CXI = 4
CYI = 4
CZ = 512
EEV_DEV = 1024
EVENTS = 8
EEV = 32768
OWNERS = 256
CAP = 256
NI_DEV = 8192
NX = 32
NY = 128
N_EV = 8
N_SP = 32


def draw_owner(key, part):
    key = jax.random.fold_in(key, 11)
    slots_total = SLOTS * EEV_DEV
    span_sp = EEV // EEV_DEV
    rows = jnp.arange(EVENTS, dtype=jnp.int32)

    def one_block(block_index):
        column = block_index % span_sp
        block_key = jax.random.fold_in(key, block_index + 1)
        first_key, second_key = jax.random.split(block_key)
        own = jnp.repeat(rows * span_sp + column, CAP)
        left = jnp.repeat(rows * span_sp + column - 1, CAP)
        right = jnp.repeat(rows * span_sp + column + 1, CAP)
        left_ok = jnp.full(left.shape, column > 0)
        right_ok = jnp.full(right.shape, column < span_sp - 1)
        supply = jnp.concatenate([left, right])
        valid = jnp.concatenate([left_ok, right_ok])
        order = jax.random.permutation(first_key, supply.shape[0])
        supply = supply[order]
        invalid = 1 - valid[order].astype(jnp.int32)
        picked = supply[jnp.argsort(invalid, stable=True)][:slots_total - own.shape[0]]
        filled = jnp.concatenate([own, picked]).astype(jnp.int32)
        return jax.random.permutation(second_key, filled)
    blocks = jax.vmap(one_block)(jnp.arange(EVENTS * span_sp, dtype=jnp.int32))
    blocks = blocks.reshape(EVENTS, span_sp, SLOTS, EEV_DEV).transpose(0, 2, 1, 3)
    return blocks.reshape(EVENTS, SLOTS, EEV).astype(jnp.int32)


def place_ends(entries, rng, low, top_value):
    place = [jax.random.randint(jax.random.fold_in(rng, axis), (), 0, length) for axis, length in enumerate(entries.shape)]
    longest = entries.shape.index(max(entries.shape))
    beside = place[:longest] + [(place[longest] + 1) % entries.shape[longest]] + place[longest + 1:]
    return entries.at[tuple(place)].set(low).at[tuple(beside)].set(top_value)


def shard_levels(own_key, shape, shards, low, high):
    def one(dim, blocks):
        draws = jax.random.uniform(jax.random.fold_in(jax.random.fold_in(own_key, 6), dim), (blocks,), jnp.float32, low / len(shards), high / len(shards))
        return jnp.repeat(jnp.exp(draws), shape[dim] // blocks).reshape((-1,) + (1,) * (len(shape) - dim - 1))

    loudness = one(*shards[0])
    for cut in shards[1:]:
        loudness = loudness * one(*cut)
    return loudness


def bell_draw(own_key, shape, scale, limit, pieces=(), kind=jnp.bfloat16):
    values = scale * jax.random.normal(own_key, shape, jnp.float32)
    if pieces:
        values = values * shard_levels(own_key, shape, pieces, -0.22, 0.18)
    return jnp.clip(values, -limit, limit).astype(kind)


def setup_inputs(seed: int = 0) -> dict:
    key_of = jax.random.split(jax.random.key(seed), 7)
    kernels = bell_draw(key_of[0], (EVENTS, PARAMS, GLL, EEV), 1.0, 6.0, ((0, 8), (3, 32)))
    basis = bell_draw(key_of[1], (NODES, GLL), GLL ** -0.5, 0.5)
    crossing = jnp.clip(jnp.exp(math.log(1.0) - 2.3025851 * jax.random.uniform(key_of[2], (EVENTS, SLOTS, EEV), jnp.float32) ** shard_levels(key_of[2], (EVENTS, SLOTS, EEV), ((0, 8), (2, 32)), -0.2, 0.2)), 0.1, 1.0)
    owner = draw_owner(jax.random.fold_in(key_of[6], 71), 0)
    target = place_ends(jax.random.randint(key_of[4], (EVENTS, SLOTS, EEV), 0, NI_DEV), jax.random.fold_in(key_of[4], 1), 0, NI_DEV - 1).astype(jnp.int32)
    diffusivity = jnp.clip(0.05 + 0.11 * jax.random.uniform(key_of[5], (NX, NY, CZ), jnp.float32) ** shard_levels(key_of[5], (NX, NY, CZ), ((0, 8), (1, 32)), -0.2, 0.2), 0.05, 0.16)
    return {"kernels": kernels, "basis": basis, "crossing": crossing, "owner": owner, "target": target, "diffusivity": diffusivity}


def diffuse(field, coeff):
    padded = jnp.pad(field, ((0, 0), (1, 1), (1, 1), (1, 1)))
    center = padded[:, 1:-1, 1:-1, 1:-1]
    total = padded[:, 2:, 1:-1, 1:-1] + padded[:, :-2, 1:-1, 1:-1]
    total = total + padded[:, 1:-1, 2:, 1:-1] + padded[:, 1:-1, :-2, 1:-1]
    total = total + padded[:, 1:-1, 1:-1, 2:] + padded[:, 1:-1, 1:-1, :-2]
    return center + coeff[None] * (total - 6.0 * center)


def reference(kernels, basis, crossing, owner, target, diffusivity):
    channels = PARAMS * NODES
    basis_wide = basis.astype(jnp.float32)

    def add_event(total, inputs):
        kernel_one, weight_one, owner_one, target_one = inputs
        projected = jnp.einsum('qg,pge->pqe', basis_wide, kernel_one.astype(jnp.float32))
        projected = projected.reshape(channels, EEV)
        contribution = projected[:, None, :] * weight_one[None]
        position = (owner_one * NI_DEV + target_one).reshape(-1)
        total = total.at[:, position].add(contribution.reshape(channels, -1))
        return total, None

    start = jnp.zeros((channels, OWNERS * NI_DEV), jnp.float32)
    total, _ = lax.scan(add_event, start, (kernels, crossing, owner, target))
    grid = total.reshape(channels, N_EV, N_SP, CXI, CYI, CZ)
    grid = grid.transpose(0, 1, 3, 2, 4, 5).reshape(channels, NX, NY, CZ)
    for step in range(STEPS):
        grid = diffuse(grid, diffusivity)
    return grid
```

```python
import jax
import jax.numpy as jnp
from jax import lax
from jax.experimental import pallas as pl
from jax.experimental.pallas import tpu as pltpu
from jax.sharding import PartitionSpec as P

MESH = pl.DeviceIdType.MESH
STEPS = 4
F32 = jnp.float32
BF16 = jnp.bfloat16
NT = (((1,), (1,)), ((), ()))


def split(value):
    high = value.astype(BF16)
    low = (value - high.astype(F32)).astype(BF16)
    return high, low


def row_ids(rows, columns, group):
    return (lax.broadcasted_iota(jnp.int32, (rows, columns), 0) // group).astype(F32).astype(BF16)


def spread(ids, row, values):
    repeats = ids.shape[0] // values.shape[0]
    wide = jnp.broadcast_to(row.astype(BF16), ids.shape)
    tiled = jnp.concatenate([values] * repeats, axis=0)
    return jnp.where(ids == wide, tiled, jnp.zeros_like(tiled))


def kernel(n_ev, n_sp, kernels, basis, crossing, owner, target, diffusivity, out,
           value_send, cell_send, value_recv, cell_recv, field, halo,
           value_out_sem, cell_out_sem, value_in_sem, cell_in_sem, halo_out_sem, halo_in_sem):
    ev = lax.axis_index("ev")
    sp = lax.axis_index("sp")
    buckets = 3 * n_ev
    slots, elements = crossing.shape[1], crossing.shape[2]
    cap = value_send.shape[3]
    has = {0: sp > 0, 1: None, 2: sp < n_sp - 1}

    def when(condition, body):
        if condition is None:
            body()
        else:
            pl.when(condition)(body)

    def peer(bucket):
        return (lax.rem(ev + bucket // 3, n_ev), sp + bucket % 3 - 1)

    barrier = pltpu.get_barrier_semaphore()
    for bucket in range(buckets):
        if bucket == 1:
            continue

        def greet(bucket=bucket):
            pl.semaphore_signal(barrier, inc=1, device_id=peer(bucket), device_id_type=MESH)
        when(has[bucket % 3], greet)

    for side, missing in ((2, sp == 0), (0, sp == n_sp - 1)):
        @pl.when(missing)
        def _(side=side):
            for q in range(n_ev):
                value_recv[3 * q + side] = jnp.zeros(value_recv.shape[1:], F32)
                cell_recv[3 * q + side] = jnp.zeros(cell_recv.shape[1:], F32)
    for face, missing in enumerate((ev == 0, ev == n_ev - 1, sp == 0, sp == n_sp - 1)):
        @pl.when(missing)
        def _(face=face):
            for t in range(STEPS):
                halo[t, face] = jnp.zeros(halo.shape[2:], F32)

    projected = [
        lax.dot_general(basis[...], kernels[0, p], (((1,), (0,)), ((), ())), preferred_element_type=F32)
        for p in range(kernels.shape[1])
    ]

    owners = owner[0]
    row = lax.rem((owners >> 5) - ev + n_ev, n_ev)
    side = (owners & (n_sp - 1)) - sp + 1
    bucket_of = (row * 3 + side).astype(F32)
    chunk = 256
    per = elements // chunk
    ids32 = lax.broadcasted_iota(jnp.int32, (32, chunk), 0).astype(F32)
    hots = []
    for k in range(slots):
        for h in range(per):
            line = bucket_of[k:k + 1, h * chunk:(h + 1) * chunk]
            hots.append(jnp.where(ids32 == line, 1.0, 0.0))
    hot = jnp.concatenate(hots, axis=0).astype(BF16)
    ri = lax.broadcasted_iota(jnp.int32, (chunk, chunk), 0)
    ci = lax.broadcasted_iota(jnp.int32, (chunk, chunk), 1)
    before = jnp.where(ri < ci, 1.0, 0.0).astype(BF16)
    prefix = jnp.dot(hot, before, preferred_element_type=F32)
    total = jnp.dot(hot, jnp.ones((chunk, chunk), BF16), preferred_element_type=F32)
    carry = jnp.zeros((32, chunk), F32)
    rank_ids = row_ids(cap, chunk, 1)
    ranks = []
    for i in range(slots * per):
        rank = jnp.sum(hots[i] * (prefix[32 * i:32 * i + 32] + carry), axis=0, keepdims=True)
        carry = carry + total[32 * i:32 * i + 32]
        wide = jnp.broadcast_to(rank.astype(BF16), rank_ids.shape)
        ranks.append(jnp.where(rank_ids == wide, jnp.ones_like(wide), jnp.zeros_like(wide)))
    ids_b = row_ids(buckets * 8, elements, 8)
    ids_c = row_ids(32, elements, 1)
    sums = [None] * 4
    for k in range(slots):
        line = bucket_of[k:k + 1, :]
        hot_rank = jnp.concatenate(ranks[k * per:(k + 1) * per], axis=1)
        hot_rank = jnp.concatenate([hot_rank, hot_rank], axis=1)
        cells = target[0, k:k + 1, :]
        for g in range(4):
            if g < 3:
                high, low = split(projected[g] * crossing[0, k:k + 1, :])
                high = jnp.concatenate([high, high], axis=0)
                low = jnp.concatenate([low, low], axis=0)
                ids = ids_b
            else:
                high = jnp.broadcast_to((cells & -256).astype(F32).astype(BF16), (16, elements))
                low = jnp.broadcast_to((cells & 255).astype(F32).astype(BF16), (16, elements))
                ids = ids_c
            left = jnp.concatenate([spread(ids, line, high), spread(ids, line, low)], axis=1)
            part = lax.dot_general(left, hot_rank, NT, preferred_element_type=F32)
            sums[g] = part if k == 0 else sums[g] + part
    for g in range(3):
        value_send[:, g] = sums[g].reshape(buckets, 8, cap)
    cell_send[...] = sums[3][:buckets].reshape(buckets, 1, cap)

    pl.semaphore_wait(barrier, n_ev - 1 + n_ev * ((sp > 0).astype(jnp.int32) + (sp < n_sp - 1).astype(jnp.int32)))
    def move(bucket):
        return [
            pltpu.make_async_remote_copy(
                src_ref=source.at[bucket], dst_ref=dest.at[bucket], send_sem=out_sem.at[bucket],
                recv_sem=in_sem.at[bucket], device_id=peer(bucket), device_id_type=MESH)
            for source, dest, out_sem, in_sem in (
                (value_send, value_recv, value_out_sem, value_in_sem),
                (cell_send, cell_recv, cell_out_sem, cell_in_sem))
        ]
    order = [0] + [q for d in range(1, n_ev // 2) for q in (d, n_ev - d)] + [n_ev // 2]
    for q in order[::-1]:
        for s in range(3):
            if q == 0 and s == 1:
                continue

            def start(bucket=3 * q + s):
                for copy in move(bucket):
                    copy.start()
            when(has[s], start)
    value_recv[1] = value_send[1]
    cell_recv[1] = cell_send[1]

    field[0] = jnp.zeros(field.shape[1:], F32)
    ids_hi = row_ids(32 * 8, cap, 8)
    ids_lo = row_ids(256, cap, 1)
    for q in order:
        hot_lo = []
        lines = []
        for s in range(3):
            bucket = 3 * q + s
            if bucket != 1:
                def arrive(bucket=bucket):
                    for copy in move(bucket):
                        copy.wait_recv()
                when(has[2 - s], arrive)
            cells = cell_recv[bucket].astype(jnp.int32)
            wide = jnp.broadcast_to((cells & 255).astype(F32).astype(BF16), ids_lo.shape)
            hot_lo.append(jnp.where(ids_lo == wide, jnp.ones_like(wide), jnp.zeros_like(wide)))
            lines.append((cells >> 8).astype(F32))
        hot_lo = jnp.concatenate(hot_lo + hot_lo, axis=1)
        for g in range(3):
            highs, lows = [], []
            for s in range(3):
                high, low = split(value_recv[3 * q + s, g])
                high = jnp.concatenate([high, high], axis=0)
                low = jnp.concatenate([low, low], axis=0)
                highs.append(spread(ids_hi, lines[s], high))
                lows.append(spread(ids_hi, lines[s], low))
            left = jnp.concatenate(highs + lows, axis=1)
            part = lax.dot_general(left, hot_lo, NT, preferred_element_type=F32)
            part = part.reshape(4, 4, 2, 8, 256)
            for z in range(2):
                field[0, g, :, :, :, z * 256:(z + 1) * 256] += part[:, :, z]

    faces = (
        (ev < n_ev - 1, ev > 0, (ev + 1, sp), lambda t, g: field.at[t, g, 3]),
        (ev > 0, ev < n_ev - 1, (ev - 1, sp), lambda t, g: field.at[t, g, 0]),
        (sp < n_sp - 1, sp > 0, (ev, sp + 1), lambda t, g: field.at[t, g, :, 3]),
        (sp > 0, sp < n_sp - 1, (ev, sp - 1), lambda t, g: field.at[t, g, :, 0]),
    )
    def face_copy(t, g, face):
        _, _, device, source = faces[face]
        return pltpu.make_async_remote_copy(
            src_ref=source(t, g), dst_ref=halo.at[t, face, g], send_sem=halo_out_sem.at[t, face, g],
            recv_sem=halo_in_sem.at[t, face, g], device_id=device, device_id_type=MESH)

    def send_faces(t, g):
        for face in range(4):
            when(faces[face][0], lambda face=face: face_copy(t, g, face).start())
    lane = lax.broadcasted_iota(jnp.int32, (32, 512), 1)
    for g in range(3):
        send_faces(0, g)
    for t in range(STEPS):
        for g in range(3):
            for face in range(4):
                when(faces[face][1], lambda face=face: face_copy(t, g, face).wait_recv())
            for a in range(4):
                center = field[t, g, a]
                above = halo[t, 0, g] if a == 0 else field[t, g, a - 1]
                below = halo[t, 1, g] if a == 3 else field[t, g, a + 1]
                around = above + below
                around += jnp.concatenate([halo[t, 2, g, a][None], center[:3]], axis=0)
                around += jnp.concatenate([center[1:], halo[t, 3, g, a][None]], axis=0)
                flat = center.reshape(32, 512)
                left = jnp.where(lane == 0, 0.0, pltpu.roll(flat, 1, 1))
                right = jnp.where(lane == 511, 0.0, pltpu.roll(flat, 511, 1))
                around += (left + right).reshape(4, 8, 512)
                coeff = diffusivity[a].reshape(4, 1, 512)
                new = center + coeff * (around - 6.0 * center)
                if t < STEPS - 1:
                    field[t + 1, g, a] = new
                else:
                    out[g, a] = new
            if t < STEPS - 1:
                send_faces(t + 1, g)

    for q in range(n_ev):
        for s in range(3):
            if q == 0 and s == 1:
                continue

            def finish(bucket=3 * q + s):
                for copy in move(bucket):
                    copy.wait_send()
            when(has[s], finish)
    for t in range(STEPS):
        for g in range(3):
            for face in range(4):
                when(faces[face][0], lambda face=face: face_copy(t, g, face).wait_send())


def solution(mesh):
    n_ev, n_sp = mesh.shape["ev"], mesh.shape["sp"]

    def per_device(kernels, basis, crossing, owner, target, diffusivity):
        import functools
        buckets = 3 * n_ev
        cap = crossing.shape[1] * crossing.shape[2] // (2 * n_ev)
        result = pl.pallas_call(
            functools.partial(kernel, n_ev, n_sp),
            out_shape=jax.ShapeDtypeStruct((3, 4, 4, 8, 512), F32),
            in_specs=[pl.BlockSpec(memory_space=pltpu.VMEM)] * 6,
            out_specs=pl.BlockSpec(memory_space=pltpu.VMEM),
            scratch_shapes=[
                pltpu.VMEM((buckets, 3, 8, cap), F32),
                pltpu.VMEM((buckets, 1, cap), F32),
                pltpu.VMEM((buckets, 3, 8, cap), F32),
                pltpu.VMEM((buckets, 1, cap), F32),
                pltpu.VMEM((STEPS, 3, 4, 4, 8, 512), F32),
                pltpu.VMEM((STEPS, 4, 3, 4, 8, 512), F32),
                pltpu.SemaphoreType.DMA((buckets,)),
                pltpu.SemaphoreType.DMA((buckets,)),
                pltpu.SemaphoreType.DMA((buckets,)),
                pltpu.SemaphoreType.DMA((buckets,)),
                pltpu.SemaphoreType.DMA((STEPS, 4, 3)),
                pltpu.SemaphoreType.DMA((STEPS, 4, 3)),
            ],
            compiler_params=pltpu.CompilerParams(
                collective_id=0, has_side_effects=True, vmem_limit_bytes=48 * 1024 * 1024),
        )(kernels, basis, crossing, owner, target, diffusivity)
        result = result.transpose(0, 3, 1, 2, 4)
        return result.reshape(24, 4, 4, 512)

    return jax.shard_map(
        per_device,
        mesh=mesh,
        in_specs=(
            P("ev", None, None, "sp"),
            P(),
            P("ev", None, "sp"),
            P("ev", None, "sp"),
            P("ev", None, "sp"),
            P("ev", "sp", None),
        ),
        out_specs=P(None, "ev", "sp", None),
        check_vma=False,
    )
```

```python
import functools

import jax
import jax.numpy as jnp
from jax import lax
from jax.experimental import pallas as pl
from jax.experimental.pallas import tpu as pltpu
from jax.sharding import PartitionSpec as P

MESH = pl.DeviceIdType.MESH
STEPS = 4
PIECES = 4
F32 = jnp.float32
BF16 = jnp.bfloat16
NN = (((1,), (0,)), ((), ()))
NT = (((1,), (1,)), ((), ()))


def split(value):
    high = value.astype(BF16)
    low = (value - high.astype(F32)).astype(BF16)
    return high, low


def twice(value):
    return jnp.concatenate([value, value], axis=0)


def row_ids(rows, columns, group):
    return (lax.broadcasted_iota(jnp.int32, (rows, columns), 0) // group).astype(F32).astype(BF16)


def spread(ids, row, values):
    repeats = ids.shape[0] // values.shape[0]
    wide = jnp.broadcast_to(row.astype(BF16), ids.shape)
    tiled = jnp.concatenate([values] * repeats, axis=0)
    return jnp.where(ids == wide, tiled, jnp.zeros_like(tiled))


def one_hot(ids, row):
    wide = jnp.broadcast_to(row.astype(BF16), ids.shape)
    return jnp.where(ids == wide, jnp.ones_like(wide), jnp.zeros_like(wide))


def when(condition, body):
    if condition is None:
        body()
    else:
        pl.when(condition)(body)


def kernel(n_ev, n_sp, *refs):
    sources, out, inputs, input_sem = refs[:6], refs[6], refs[7:13], refs[13]
    loads = [pltpu.make_async_copy(sources[i], inputs[i], input_sem.at[i]) for i in range(6)]
    for i in (1, 0, 3, 4, 2, 5):
        loads[i].start()
    body(n_ev, n_sp, loads, *inputs, out, *refs[14:])


def body(n_ev, n_sp, loads, kernels, basis, crossing, owner, target, diffusivity, out,
         raw, lists, side_lists, field, halo,
         ring_out_sem, ring_in_sem, side_out_sem, side_in_sem, list_out_sem, list_in_sem,
         side_list_out_sem, side_list_in_sem,
         halo_out_sem, halo_in_sem):
    ev = lax.axis_index("ev")
    sp = lax.axis_index("sp")
    buckets = 3 * n_ev
    slots, elements = crossing.shape[1], crossing.shape[2]
    cap = lists.shape[5]
    piece = elements // PIECES
    half = n_ev // 2
    has = {0: sp > 0, 1: None, 2: sp < n_sp - 1}

    def beside(s):
        return (ev, sp + s - 1)

    def along(up):
        return (lax.rem(ev + (1 if up else n_ev - 1), n_ev), sp)

    barrier = pltpu.get_barrier_semaphore()
    for up in (True, False):
        pl.semaphore_signal(barrier, inc=1, device_id=along(up), device_id_type=MESH)
    for s in (0, 2):
        when(has[s], lambda s=s: pl.semaphore_signal(barrier, inc=1, device_id=beside(s), device_id_type=MESH))

    for s, missing in ((2, sp == 0), (0, sp == n_sp - 1)):
        @pl.when(missing)
        def _(s=s):
            raw[2 - s] = jnp.zeros(raw.shape[1:], F32)
            side_lists[s // 2] = jnp.zeros(side_lists.shape[1:], F32)
    for face, missing in enumerate((ev == 0, ev == n_ev - 1, sp == 0, sp == n_sp - 1)):
        @pl.when(missing)
        def _(face=face):
            for t in range(STEPS):
                halo[t, face] = jnp.zeros(halo.shape[2:], F32)

    loads[1].wait()
    loads[0].wait()
    for p in range(kernels.shape[1]):
        part = lax.dot_general(basis[...], kernels[0, p], NN, preferred_element_type=F32)
        for h in range(PIECES):
            raw[1, 0, h, 8 * p:8 * p + 8] = part[:, h * piece:(h + 1) * piece]

    def ring(q, h, up):
        to = (q + 1 if up else q - 1) % n_ev
        return pltpu.make_async_remote_copy(
            src_ref=raw.at[1, q, h], dst_ref=raw.at[1, to, h], send_sem=ring_out_sem.at[int(up), q, h],
            recv_sem=ring_in_sem.at[to, h], device_id=along(up), device_id_type=MESH)

    def ring_pieces(q, up):
        last = half - 1 if up else half + 1
        if q == half or (q != 0 and up != (q < half)):
            return ()
        if q != last:
            return range(PIECES)
        return range(PIECES // 2) if up else range(PIECES // 2, PIECES)

    def sideways(q, s):
        return pltpu.make_async_remote_copy(
            src_ref=raw.at[1, q], dst_ref=raw.at[2 - s, q], send_sem=side_out_sem.at[s // 2, q],
            recv_sem=side_in_sem.at[s // 2, q], device_id=beside(s), device_id_type=MESH)

    def arrive(places):
        for h in range(PIECES):
            for q in places:
                up = q < half
                if q == half:
                    up = h < PIECES // 2
                ring((q - 1 if up else q + 1) % n_ev, h, up).wait_recv()
                if h in ring_pieces(q, up):
                    ring(q, h, up).start()
        for q in places:
            for s in (0, 2):
                when(has[s], lambda q=q, s=s: sideways(q, s).start())

    def pass_lists(q, up):
        to = (q + 1 if up else q - 1) % n_ev
        rows = pl.ds(q + 1, half - q) if up else pl.ds(half + 1, (q or n_ev) - half - 1)
        return pltpu.make_async_remote_copy(
            src_ref=lists.at[q, rows], dst_ref=lists.at[to, rows], send_sem=list_out_sem.at[int(up), q],
            recv_sem=list_in_sem.at[to], device_id=along(up), device_id_type=MESH)

    def pass_lists_to(q):
        return [up for up in (True, False) if (q == 0) or (q < half if up else q > half + 1) and up == (q < half)]

    def lists_sideways(q, s):
        return pltpu.make_async_remote_copy(
            src_ref=lists.at[q, q, s], dst_ref=side_lists.at[s // 2, q], send_sem=side_list_out_sem.at[s // 2, q],
            recv_sem=side_list_in_sem.at[s // 2, q], device_id=beside(s), device_id_type=MESH)

    def arrive_lists(places):
        for q in places:
            up = q <= half
            if q != 0:
                pass_lists((q - 1 if up else q + 1) % n_ev, up).wait_recv()
            for up in pass_lists_to(q):
                pass_lists(q, up).start()
        for q in places:
            for s in (0, 2):
                when(has[s], lambda q=q, s=s: lists_sideways(q, s).start())

    pl.semaphore_wait(barrier, 2 + (sp > 0).astype(jnp.int32) + (sp < n_sp - 1).astype(jnp.int32))
    for h in range(PIECES):
        for up in (True, False):
            ring(0, h, up).start()
    for s in (0, 2):
        when(has[s], lambda s=s: sideways(0, s).start())

    loads[3].wait()
    owners = owner[0]
    row = lax.rem((owners >> 5) - ev + n_ev, n_ev)
    side = (owners & (n_sp - 1)) - sp + 1
    bucket_of = (row * 3 + side).astype(F32)
    chunk = 256
    per = elements // chunk
    ids_f32 = lax.broadcasted_iota(jnp.int32, (32, chunk), 0).astype(F32)
    hots = []
    for k in range(slots):
        for h in range(per):
            line = bucket_of[k:k + 1, h * chunk:(h + 1) * chunk]
            hots.append(jnp.where(ids_f32 == line, 1.0, 0.0))
    hot = jnp.concatenate(hots, axis=0).astype(BF16)
    ri = lax.broadcasted_iota(jnp.int32, (chunk, chunk), 0)
    ci = lax.broadcasted_iota(jnp.int32, (chunk, chunk), 1)
    before = jnp.where(ri < ci, 1.0, 0.0).astype(BF16)
    prefix = jnp.dot(hot, before, preferred_element_type=F32)
    total = jnp.dot(hot, jnp.ones((chunk, chunk), BF16), preferred_element_type=F32)
    carry = jnp.zeros((32, chunk), F32)
    ids_cap = row_ids(cap, chunk, 1)
    ranks = []
    for i in range(slots * per):
        rank = jnp.sum(hots[i] * (prefix[32 * i:32 * i + 32] + carry), axis=0, keepdims=True)
        carry = carry + total[32 * i:32 * i + 32]
        ranks.append(one_hot(ids_cap, rank))
    loads[4].wait()
    loads[2].wait()
    ids_bucket = row_ids(32, elements, 1)
    element = lax.broadcasted_iota(jnp.int32, (1, elements), 1)
    sums = None
    for k in range(slots):
        line = bucket_of[k:k + 1, :]
        hot_rank = jnp.concatenate(ranks[k * per:(k + 1) * per], axis=1)
        cells = target[0, k:k + 1, :]
        high, low = split(crossing[0, k:k + 1, :])
        parts = [
            (element & -16).astype(F32).astype(BF16), high, (cells & -256).astype(F32).astype(BF16),
            (element & 15).astype(F32).astype(BF16), low, (cells & 255).astype(F32).astype(BF16),
        ]
        left = jnp.concatenate(
            [spread(ids_bucket, line, jnp.broadcast_to(x.astype(F32), (16, elements)).astype(BF16)) for x in parts],
            axis=0)
        part = lax.dot_general(left, hot_rank, NT, preferred_element_type=F32)
        sums = part if k == 0 else sums + part
    sums = sums[:96] + sums[96:]
    for kind in range(3):
        lists[0, :, :, kind] = sums[32 * kind:32 * kind + buckets].reshape(n_ev, 3, 1, cap)
    arrive_lists((0,))

    ids_hi = row_ids(32 * 8, cap, 8)
    ids_lo = row_ids(256, cap, 1)

    def collect(q, done=None):
        hots, lines, values = [], [], []
        for s in (1, 0, 2):
            if s != 1:
                when(has[2 - s], lambda q=q, s=s: lists_sideways(q, s).wait_recv())
                when(has[2 - s], lambda q=q, s=s: sideways(q, s).wait_recv())
            listed = lists[q, q, 1] if s == 1 else side_lists[s // 2, q]
            source = jnp.concatenate([raw[2 - s, q, h] for h in range(PIECES)], axis=1)
            high = source.astype(BF16).astype(F32)
            source = jnp.concatenate([high, source - high], axis=0).astype(BF16)
            chosen = listed[0]
            pick = jnp.concatenate(
                [one_hot(ids_lo, chosen - 256.0 * i) for i in range(elements // 256)], axis=0)
            value = lax.dot_general(source, pick, NN, preferred_element_type=F32)
            values.append((value[:24] + value[24:]) * listed[1])
            cells = listed[2].astype(jnp.int32)
            hots.append(one_hot(ids_lo, (cells & 255).astype(F32)))
            lines.append((cells >> 8).astype(F32))
        right = jnp.concatenate(hots, axis=1)
        for g in range(3):
            highs, lows = [], []
            for value, line in zip(values, lines):
                high, low = split(value[8 * g:8 * g + 8])
                highs.append(spread(ids_hi, line, twice(high)))
                lows.append(spread(ids_hi, line, twice(low)))
            left = jnp.concatenate([jnp.concatenate(highs, axis=1), jnp.concatenate(lows, axis=1)], axis=0)
            part = lax.dot_general(left, right, NT, preferred_element_type=F32)
            part = (part[:256] + part[256:]).reshape(4, 4, 2, 8, 256)
            for z in range(2):
                lanes = slice(z * 256, (z + 1) * 256)
                if q == 0:
                    field[0, g, :, :, :, lanes] = part[:, :, z]
                else:
                    field[0, g, :, :, :, lanes] += part[:, :, z]
            if done is not None:
                done(g)

    faces = (
        (ev < n_ev - 1, ev > 0, (ev + 1, sp), lambda t, g: field.at[t, g, 3]),
        (ev > 0, ev < n_ev - 1, (ev - 1, sp), lambda t, g: field.at[t, g, 0]),
        (sp < n_sp - 1, sp > 0, (ev, sp + 1), lambda t, g: field.at[t, g, :, 3]),
        (sp > 0, sp < n_sp - 1, (ev, sp - 1), lambda t, g: field.at[t, g, :, 0]),
    )

    def face_copy(t, g, face):
        _, _, device, source = faces[face]
        return pltpu.make_async_remote_copy(
            src_ref=source(t, g), dst_ref=halo.at[t, face, g], send_sem=halo_out_sem.at[t, face, g],
            recv_sem=halo_in_sem.at[t, face, g], device_id=device, device_id_type=MESH)

    def send_faces(t, g):
        for face in range(4):
            when(faces[face][0], lambda face=face: face_copy(t, g, face).start())

    lane = lax.broadcasted_iota(jnp.int32, (32, 512), 1)

    def step(t, g):
        for face in range(4):
            when(faces[face][1], lambda face=face: face_copy(t, g, face).wait_recv())
        for a in range(4):
            center = field[t, g, a]
            above = halo[t, 0, g] if a == 0 else field[t, g, a - 1]
            below = halo[t, 1, g] if a == 3 else field[t, g, a + 1]
            around = above + below
            around += jnp.concatenate([halo[t, 2, g, a][None], center[:3]], axis=0)
            around += jnp.concatenate([center[1:], halo[t, 3, g, a][None]], axis=0)
            flat = center.reshape(32, 512)
            left = jnp.where(lane == 0, 0.0, pltpu.roll(flat, 1, 1))
            right = jnp.where(lane == 511, 0.0, pltpu.roll(flat, 511, 1))
            around += (left + right).reshape(4, 8, 512)
            coeff = diffusivity[a].reshape(4, 1, 512)
            new = center + coeff * (around - 6.0 * center)
            if t < STEPS - 1:
                field[t + 1, g, a] = new
            else:
                for b2 in range(4):
                    for zt in range(4):
                        rows = pl.ds(g * 512 + a * 16 + zt * 4 + b2, 8, stride=64)
                        out[rows, :] = new[b2, :, zt * 128:(zt + 1) * 128]
        if t < STEPS - 1:
            send_faces(t + 1, g)

    arrive((1, n_ev - 1))
    arrive_lists((1, n_ev - 1))
    collect(0)
    arrive((2, n_ev - 2))
    arrive_lists((2, n_ev - 2))
    collect(1)
    collect(n_ev - 1)
    arrive((3, n_ev - 3))
    arrive_lists((3, n_ev - 3))
    collect(2)
    arrive((half,))
    arrive_lists((half,))
    collect(n_ev - 2)
    collect(3)
    collect(n_ev - 3)
    collect(half, lambda g: send_faces(0, g))
    loads[5].wait()
    for t in range(STEPS):
        for g in range(3):
            step(t, g)

    for q in range(n_ev):
        for up in pass_lists_to(q):
            pass_lists(q, up).wait_send()
        for up in (True, False):
            for h in ring_pieces(q, up):
                ring(q, h, up).wait_send()
        for s in (0, 2):
            when(has[s], lambda q=q, s=s: lists_sideways(q, s).wait_send())
            when(has[s], lambda q=q, s=s: sideways(q, s).wait_send())
    for t in range(STEPS):
        for g in range(3):
            for face in range(4):
                when(faces[face][0], lambda face=face: face_copy(t, g, face).wait_send())


def solution(mesh):
    n_ev, n_sp = mesh.shape["ev"], mesh.shape["sp"]

    def per_device(*arguments):
        crossing = arguments[2]
        elements = crossing.shape[2]
        cap = crossing.shape[1] * elements // (2 * n_ev)
        arguments = [pltpu.with_memory_space_constraint(x, pltpu.HBM) for x in arguments]
        result = pl.pallas_call(
            functools.partial(kernel, n_ev, n_sp),
            out_shape=jax.ShapeDtypeStruct((1536, 128), F32),
            in_specs=[pl.BlockSpec(memory_space=pl.ANY)] * 6,
            out_specs=pl.BlockSpec(memory_space=pltpu.VMEM),
            scratch_shapes=[
                *[pltpu.VMEM(x.shape, x.dtype) for x in arguments],
                pltpu.SemaphoreType.DMA((6,)),
                pltpu.VMEM((3, n_ev, PIECES, 24, elements // PIECES), F32),
                pltpu.VMEM((n_ev, n_ev, 3, 3, 1, cap), F32),
                pltpu.VMEM((2, n_ev, 3, 1, cap), F32),
                pltpu.VMEM((STEPS, 3, 4, 4, 8, 512), F32),
                pltpu.VMEM((STEPS, 4, 3, 4, 8, 512), F32),
                pltpu.SemaphoreType.DMA((2, n_ev, PIECES)),
                pltpu.SemaphoreType.DMA((n_ev, PIECES)),
                pltpu.SemaphoreType.DMA((2, n_ev)),
                pltpu.SemaphoreType.DMA((2, n_ev)),
                pltpu.SemaphoreType.DMA((2, n_ev)),
                pltpu.SemaphoreType.DMA((n_ev,)),
                pltpu.SemaphoreType.DMA((2, n_ev)),
                pltpu.SemaphoreType.DMA((2, n_ev)),
                pltpu.SemaphoreType.DMA((STEPS, 4, 3)),
                pltpu.SemaphoreType.DMA((STEPS, 4, 3)),
            ],
            compiler_params=pltpu.CompilerParams(
                collective_id=0, has_side_effects=True, vmem_limit_bytes=40 * 1024 * 1024),
        )(*arguments)
        result = result.reshape(24, 4, 4, 4, 128).transpose(0, 1, 3, 2, 4)
        return result.reshape(24, 4, 4, 512)

    return jax.shard_map(
        per_device,
        mesh=mesh,
        in_specs=(
            P("ev", None, None, "sp"),
            P(),
            P("ev", None, "sp"),
            P("ev", None, "sp"),
            P("ev", None, "sp"),
            P("ev", "sp", None),
        ),
        out_specs=P(None, "ev", "sp", None),
        check_vma=False,
    )
```

```python
import jax
import jax.numpy as jnp
from jax import lax
from jax.experimental import pallas as pl
from jax.experimental.pallas import tpu as pltpu
from jax.sharding import PartitionSpec as P

MESH = pl.DeviceIdType.MESH
STEPS = 4
F32 = jnp.float32
BF16 = jnp.bfloat16
NT = (((1,), (1,)), ((), ()))


def split(value):
    high = value.astype(BF16)
    low = (value - high.astype(F32)).astype(BF16)
    return high, low


def row_ids(rows, columns, group):
    return (lax.broadcasted_iota(jnp.int32, (rows, columns), 0) // group).astype(F32).astype(BF16)


def spread(ids, row, values):
    repeats = ids.shape[0] // values.shape[0]
    wide = jnp.broadcast_to(row.astype(BF16), ids.shape)
    tiled = jnp.concatenate([values] * repeats, axis=0)
    return jnp.where(ids == wide, tiled, jnp.zeros_like(tiled))


def kernel(n_ev, n_sp, *refs):
    sources, out, inputs, input_sem = refs[:6], refs[6], refs[7:13], refs[13]
    loads = [pltpu.make_async_copy(sources[i], inputs[i], input_sem.at[i]) for i in range(6)]
    for i in (3, 4, 0, 1, 2, 5):
        loads[i].start()
    body(n_ev, n_sp, loads, *inputs, out, *refs[14:])


def body(n_ev, n_sp, loads, kernels, basis, crossing, owner, target, diffusivity, out,
           value_send, cell_send, value_recv, cell_recv, field, halo, hot_lo,
           value_out_sem, cell_out_sem, value_in_sem, cell_in_sem, halo_out_sem, halo_in_sem):
    ev = lax.axis_index("ev")
    sp = lax.axis_index("sp")
    buckets = 3 * n_ev
    slots, elements = crossing.shape[1], crossing.shape[2]
    cap = value_send.shape[3]
    has = {0: sp > 0, 1: None, 2: sp < n_sp - 1}

    def when(condition, body):
        if condition is None:
            body()
        else:
            pl.when(condition)(body)

    def peer(bucket):
        return (lax.rem(ev + bucket // 3, n_ev), sp + bucket % 3 - 1)

    barrier = pltpu.get_barrier_semaphore()
    for bucket in range(buckets):
        if bucket == 1:
            continue

        def greet(bucket=bucket):
            pl.semaphore_signal(barrier, inc=1, device_id=peer(bucket), device_id_type=MESH)
        when(has[bucket % 3], greet)

    for side, missing in ((2, sp == 0), (0, sp == n_sp - 1)):
        @pl.when(missing)
        def _(side=side):
            for q in range(n_ev):
                value_recv[:, 3 * q + side] = jnp.zeros((3,) + value_recv.shape[2:], F32)
                cell_recv[3 * q + side] = jnp.zeros(cell_recv.shape[1:], F32)
    for face, missing in enumerate((ev == 0, ev == n_ev - 1, sp == 0, sp == n_sp - 1)):
        @pl.when(missing)
        def _(face=face):
            for t in range(STEPS):
                halo[t, face] = jnp.zeros(halo.shape[2:], F32)

    loads[3].wait()
    owners = owner[0]
    row = lax.rem((owners >> 5) - ev + n_ev, n_ev)
    side = (owners & (n_sp - 1)) - sp + 1
    bucket_of = (row * 3 + side).astype(F32)
    chunk = 256
    per = elements // chunk
    ids32 = lax.broadcasted_iota(jnp.int32, (32, chunk), 0).astype(F32)
    hots = []
    for k in range(slots):
        for h in range(per):
            line = bucket_of[k:k + 1, h * chunk:(h + 1) * chunk]
            hots.append(jnp.where(ids32 == line, 1.0, 0.0))
    hot = jnp.concatenate(hots, axis=0).astype(BF16)
    ri = lax.broadcasted_iota(jnp.int32, (chunk, chunk), 0)
    ci = lax.broadcasted_iota(jnp.int32, (chunk, chunk), 1)
    before = jnp.where(ri < ci, 1.0, 0.0).astype(BF16)
    prefix = jnp.dot(hot, before, preferred_element_type=F32)
    total = jnp.dot(hot, jnp.ones((chunk, chunk), BF16), preferred_element_type=F32)
    carry = jnp.zeros((32, chunk), F32)
    rank_ids = row_ids(cap, chunk, 1)
    ranks = []
    for i in range(slots * per):
        rank = jnp.sum(hots[i] * (prefix[32 * i:32 * i + 32] + carry), axis=0, keepdims=True)
        carry = carry + total[32 * i:32 * i + 32]
        wide = jnp.broadcast_to(rank.astype(BF16), rank_ids.shape)
        ranks.append(jnp.where(rank_ids == wide, jnp.ones_like(wide), jnp.zeros_like(wide)))
    def bucket(group):
        total = None
        for k in range(slots):
            line = bucket_of[k:k + 1, :]
            hot_rank = jnp.concatenate(ranks[k * per:(k + 1) * per], axis=1)
            if group is None:
                cells = target[0, k:k + 1, :]
                high = jnp.broadcast_to((cells & -256).astype(F32).astype(BF16), (16, elements))
                low = jnp.broadcast_to((cells & 255).astype(F32).astype(BF16), (16, elements))
                ids = row_ids(32, elements, 1)
            else:
                high, low = split(projected[group] * crossing[0, k:k + 1, :])
                high = jnp.concatenate([high, high], axis=0)
                low = jnp.concatenate([low, low], axis=0)
                ids = row_ids(buckets * 8, elements, 8)
            left = jnp.concatenate([spread(ids, line, high), spread(ids, line, low)], axis=0)
            part = lax.dot_general(left, hot_rank, NT, preferred_element_type=F32)
            total = part if k == 0 else total + part
        total = total[:total.shape[0] // 2] + total[total.shape[0] // 2:]
        if group is None:
            cell_send[...] = total[:buckets].reshape(buckets, 1, cap)
        else:
            value_send[group] = total.reshape(buckets, 8, cap)

    def move(bucket, group):
        source, dest, out_sem, in_sem = (
            (cell_send, cell_recv, cell_out_sem, cell_in_sem) if group is None else
            (value_send.at[group], value_recv.at[group], value_out_sem.at[group], value_in_sem.at[group]))
        return pltpu.make_async_remote_copy(
            src_ref=source.at[bucket], dst_ref=dest.at[bucket], send_sem=out_sem.at[bucket],
            recv_sem=in_sem.at[bucket], device_id=peer(bucket), device_id_type=MESH)

    order = [0] + [q for d in range(1, n_ev // 2) for q in (d, n_ev - d)] + [n_ev // 2]

    def send(group):
        for q in order:
            for s in range(3):
                if 3 * q + s != 1:
                    when(has[s], lambda b=3 * q + s: move(b, group).start())
        if group is None:
            cell_recv[1] = cell_send[1]
        else:
            value_recv[group, 1] = value_send[group, 1]

    for i in (0, 1, 2):
        loads[i].wait()
    projected = [
        lax.dot_general(basis[...], kernels[0, p], (((1,), (0,)), ((), ())), preferred_element_type=F32)
        for p in range(kernels.shape[1])
    ]

    def sent(group):
        for b in range(buckets):
            if b != 1:
                when(has[b % 3], lambda b=b: move(b, group).wait_send())

    bucket(0)
    pl.semaphore_wait(barrier, n_ev - 1 + n_ev * ((sp > 0).astype(jnp.int32) + (sp < n_sp - 1).astype(jnp.int32)))
    send(0)
    loads[4].wait()
    bucket(None)
    send(None)
    loads[5].wait()

    ids_hi = row_ids(32 * 8, cap, 8)
    ids_lo = row_ids(256, cap, 1)

    def scatter(group):
        field[0, group] = jnp.zeros(field.shape[2:], F32)
        for q in order:
            highs, lows = [], []
            for s in range(3):
                b = 3 * q + s
                if b != 1:
                    when(has[2 - s], lambda b=b: move(b, group).wait_recv())
                    if group == 0:
                        when(has[2 - s], lambda b=b: move(b, None).wait_recv())
                cells = cell_recv[b].astype(jnp.int32)
                if group == 0:
                    wide = jnp.broadcast_to((cells & 255).astype(F32).astype(BF16), ids_lo.shape)
                    hot_lo[q, :, s * cap:(s + 1) * cap] = jnp.where(
                        ids_lo == wide, jnp.ones_like(wide), jnp.zeros_like(wide))
                line = (cells >> 8).astype(F32)
                high, low = split(value_recv[group, b])
                high = jnp.concatenate([high, high], axis=0)
                low = jnp.concatenate([low, low], axis=0)
                highs.append(spread(ids_hi, line, high))
                lows.append(spread(ids_hi, line, low))
            right = hot_lo[q]
            left = jnp.concatenate(highs + lows, axis=1)
            part = lax.dot_general(left, jnp.concatenate([right, right], axis=1), NT, preferred_element_type=F32)
            part = part.reshape(4, 4, 2, 8, 256)
            for z in range(2):
                field[0, group, :, :, :, z * 256:(z + 1) * 256] += part[:, :, z]

    faces = (
        (ev < n_ev - 1, ev > 0, (ev + 1, sp), lambda t, g: field.at[t, g, 3]),
        (ev > 0, ev < n_ev - 1, (ev - 1, sp), lambda t, g: field.at[t, g, 0]),
        (sp < n_sp - 1, sp > 0, (ev, sp + 1), lambda t, g: field.at[t, g, :, 3]),
        (sp > 0, sp < n_sp - 1, (ev, sp - 1), lambda t, g: field.at[t, g, :, 0]),
    )
    def face_copy(t, g, face):
        _, _, device, source = faces[face]
        return pltpu.make_async_remote_copy(
            src_ref=source(t, g), dst_ref=halo.at[t, face, g], send_sem=halo_out_sem.at[t, face, g],
            recv_sem=halo_in_sem.at[t, face, g], device_id=device, device_id_type=MESH)

    def send_faces(t, g, which=range(4)):
        for face in which:
            when(faces[face][0], lambda face=face: face_copy(t, g, face).start())

    lane = lax.broadcasted_iota(jnp.int32, (32, 512), 1)
    def step(t, g):
        for face in range(4):
            when(faces[face][1], lambda face=face: face_copy(t, g, face).wait_recv())
        for a in (0, 3, 1, 2):
            center = field[t, g, a]
            above = halo[t, 0, g] if a == 0 else field[t, g, a - 1]
            below = halo[t, 1, g] if a == 3 else field[t, g, a + 1]
            around = above + below
            around += jnp.concatenate([halo[t, 2, g, a][None], center[:3]], axis=0)
            around += jnp.concatenate([center[1:], halo[t, 3, g, a][None]], axis=0)
            flat = center.reshape(32, 512)
            left = jnp.where(lane == 0, 0.0, pltpu.roll(flat, 1, 1))
            right = jnp.where(lane == 511, 0.0, pltpu.roll(flat, 511, 1))
            around += (left + right).reshape(4, 8, 512)
            coeff = diffusivity[a].reshape(4, 1, 512)
            new = center + coeff * (around - 6.0 * center)
            if t < STEPS - 1:
                field[t + 1, g, a] = new
                if a in (0, 3):
                    send_faces(t + 1, g, (1 if a == 0 else 0,))
            else:
                for b2 in range(4):
                    for zt in range(4):
                        out[pl.ds(g * 512 + a * 16 + zt * 4 + b2, 8, stride=64), :] = new[b2, :, zt * 128:(zt + 1) * 128]
        if t < STEPS - 1:
            send_faces(t + 1, g, (2, 3))

    bucket(1)
    bucket(2)
    sent(0)
    send(1)
    send(2)
    scatter(0)
    send_faces(0, 0)
    scatter(1)
    send_faces(0, 1)
    scatter(2)
    send_faces(0, 2)
    for t in range(STEPS):
        for g in range(3):
            step(t, g)

    for group in (None, 1, 2,):
        sent(group)
    for t in range(STEPS):
        for g in range(3):
            for face in range(4):
                when(faces[face][0], lambda face=face: face_copy(t, g, face).wait_send())


def solution(mesh):
    n_ev, n_sp = mesh.shape["ev"], mesh.shape["sp"]

    def per_device(kernels, basis, crossing, owner, target, diffusivity):
        import functools
        buckets = 3 * n_ev
        cap = crossing.shape[1] * crossing.shape[2] // (2 * n_ev)
        arguments = [pltpu.with_memory_space_constraint(x, pltpu.HBM) for x in (kernels, basis, crossing, owner, target, diffusivity)]
        result = pl.pallas_call(
            functools.partial(kernel, n_ev, n_sp),
            out_shape=jax.ShapeDtypeStruct((1536, 128), F32),
            in_specs=[pl.BlockSpec(memory_space=pl.ANY)] * 6,
            out_specs=pl.BlockSpec(memory_space=pltpu.VMEM),
            scratch_shapes=[
                *[pltpu.VMEM(x.shape, x.dtype) for x in arguments],
                pltpu.SemaphoreType.DMA((6,)),
                pltpu.VMEM((3, buckets, 8, cap), F32),
                pltpu.VMEM((buckets, 1, cap), F32),
                pltpu.VMEM((3, buckets, 8, cap), F32),
                pltpu.VMEM((buckets, 1, cap), F32),
                pltpu.VMEM((STEPS, 3, 4, 4, 8, 512), F32),
                pltpu.VMEM((STEPS, 4, 3, 4, 8, 512), F32),
                pltpu.VMEM((n_ev, 256, 3 * cap), BF16),
                pltpu.SemaphoreType.DMA((3, buckets)),
                pltpu.SemaphoreType.DMA((buckets,)),
                pltpu.SemaphoreType.DMA((3, buckets)),
                pltpu.SemaphoreType.DMA((buckets,)),
                pltpu.SemaphoreType.DMA((STEPS, 4, 3)),
                pltpu.SemaphoreType.DMA((STEPS, 4, 3)),
            ],
            compiler_params=pltpu.CompilerParams(
                collective_id=0, has_side_effects=True, vmem_limit_bytes=40 * 1024 * 1024),
        )(*arguments)
        result = result.reshape(24, 4, 4, 4, 128).transpose(0, 1, 3, 2, 4)
        return result.reshape(24, 4, 4, 512)

    return jax.shard_map(
        per_device,
        mesh=mesh,
        in_specs=(
            P("ev", None, None, "sp"),
            P(),
            P("ev", None, "sp"),
            P("ev", None, "sp"),
            P("ev", None, "sp"),
            P("ev", "sp", None),
        ),
        out_specs=P(None, "ev", "sp", None),
        check_vma=False,
    )
```

```python
import jax
import jax.numpy as jnp
from jax import lax
from jax.experimental import pallas as pl
from jax.experimental.pallas import tpu as pltpu
from jax.sharding import PartitionSpec as P

MESH = pl.DeviceIdType.MESH
STEPS = 4
F32 = jnp.float32
BF16 = jnp.bfloat16
NT = (((1,), (1,)), ((), ()))


def split(value):
    high = value.astype(BF16)
    low = (value - high.astype(F32)).astype(BF16)
    return high, low


def row_ids(rows, columns, group):
    return (lax.broadcasted_iota(jnp.int32, (rows, columns), 0) // group).astype(F32).astype(BF16)


def spread(ids, row, values):
    repeats = ids.shape[0] // values.shape[0]
    wide = jnp.broadcast_to(row.astype(BF16), ids.shape)
    tiled = jnp.concatenate([values] * repeats, axis=0)
    return jnp.where(ids == wide, tiled, jnp.zeros_like(tiled))


def kernel(n_ev, n_sp, *refs):
    sources, out, inputs, input_sem = refs[:6], refs[6], refs[7:13], refs[13]
    loads = [pltpu.make_async_copy(sources[i], inputs[i], input_sem.at[i]) for i in range(1, 6)]
    loads += [pltpu.make_async_copy(sources[0].at[:, p], inputs[0].at[:, p], input_sem.at[6 + p]) for p in range(3)]
    for i in (2, 0, 5, 1, 6, 7, 3, 4):
        loads[i].start()
    body(n_ev, n_sp, loads, *inputs, out, *refs[14:])


def body(n_ev, n_sp, loads, kernels, basis, crossing, owner, target, diffusivity, out,
           value_send, cell_send, value_recv, cell_recv, field, halo, hot_lo,
           value_out_sem, cell_out_sem, value_in_sem, cell_in_sem, halo_out_sem, halo_in_sem):
    ev = lax.axis_index("ev")
    sp = lax.axis_index("sp")
    buckets = 3 * n_ev
    slots, elements = crossing.shape[1], crossing.shape[2]
    cap = value_send.shape[3]
    has = {0: sp > 0, 1: None, 2: sp < n_sp - 1}

    def when(condition, body):
        if condition is None:
            body()
        else:
            pl.when(condition)(body)

    inside = jnp.logical_and(sp > 0, sp < n_sp - 1)

    def each(pairs, act):
        @pl.when(inside)
        def _():
            for q, s in pairs:
                act(q, s)

        @pl.when(jnp.logical_not(inside))
        def _():
            for q, s in pairs:
                when(has[s], lambda q=q, s=s: act(q, s))

    def peer(bucket):
        return (lax.rem(ev + bucket // 3, n_ev), sp + bucket % 3 - 1)

    barrier = pltpu.get_barrier_semaphore()
    distant = [half for d in range(1, n_ev // 2) for half in (n_ev - d, d)]
    each([(q, s) for q in [n_ev // 2] + distant[::-1] + [0] for s in range(3) if 3 * q + s != 1], lambda q, s: pl.semaphore_signal(
        barrier, inc=1, device_id=peer(3 * q + s), device_id_type=MESH))

    for side, missing in ((2, sp == 0), (0, sp == n_sp - 1)):
        @pl.when(missing)
        def _(side=side):
            for q in range(n_ev):
                value_recv[:, 3 * q + side] = jnp.zeros((3,) + value_recv.shape[2:], F32)
                cell_recv[3 * q + side] = jnp.zeros(cell_recv.shape[1:], F32)
    for face, missing in enumerate((ev == 0, ev == n_ev - 1, sp == 0, sp == n_sp - 1)):
        @pl.when(missing)
        def _(face=face):
            for t in range(STEPS):
                halo[t, face] = jnp.zeros(halo.shape[2:], F32)

    loads[2].wait()
    owners = owner[0]
    row = lax.rem((owners >> 5) - ev + n_ev, n_ev)
    side = (owners & (n_sp - 1)) - sp + 1
    bucket_of = (row * 3 + side).astype(F32)
    chunk = 256
    per = elements // chunk
    ids32 = lax.broadcasted_iota(jnp.int32, (32, chunk), 0).astype(F32)
    hots = []
    for k in range(slots):
        for h in range(per):
            line = bucket_of[k:k + 1, h * chunk:(h + 1) * chunk]
            hots.append(jnp.where(ids32 == line, 1.0, 0.0))
    hot = jnp.concatenate(hots, axis=0).astype(BF16)
    ri = lax.broadcasted_iota(jnp.int32, (chunk, chunk), 0)
    ci = lax.broadcasted_iota(jnp.int32, (chunk, chunk), 1)
    before = jnp.where(ri < ci, 1.0, 0.0).astype(BF16)
    prefix = jnp.dot(hot, before, preferred_element_type=F32)
    total = jnp.dot(hot, jnp.ones((chunk, chunk), BF16), preferred_element_type=F32)
    carry = jnp.zeros((32, chunk), F32)
    rank_ids = row_ids(cap, chunk, 1)
    ranks = []
    for i in range(slots * per):
        rank = jnp.sum(hots[i] * (prefix[32 * i:32 * i + 32] + carry), axis=0, keepdims=True)
        carry = carry + total[32 * i:32 * i + 32]
        wide = jnp.broadcast_to(rank.astype(BF16), rank_ids.shape)
        ranks.append(jnp.where(rank_ids == wide, jnp.ones_like(wide), jnp.zeros_like(wide)))
    def bucket(group):
        total = None
        for k in range(slots):
            line = bucket_of[k:k + 1, :]
            hot_rank = jnp.concatenate(ranks[k * per:(k + 1) * per], axis=1)
            if group is None:
                cells = target[0, k:k + 1, :]
                high = jnp.broadcast_to((cells & -256).astype(F32).astype(BF16), (16, elements))
                low = jnp.broadcast_to((cells & 255).astype(F32).astype(BF16), (16, elements))
                ids = row_ids(32, elements, 1)
            else:
                high, low = split(projected[group] * crossing[0, k:k + 1, :])
                high = jnp.concatenate([high, high], axis=0)
                low = jnp.concatenate([low, low], axis=0)
                ids = row_ids(buckets * 8, elements, 8)
            left = jnp.concatenate([spread(ids, line, high), spread(ids, line, low)], axis=0)
            part = lax.dot_general(left, hot_rank, NT, preferred_element_type=F32)
            total = part if k == 0 else total + part
        total = total[:total.shape[0] // 2] + total[total.shape[0] // 2:]
        if group is None:
            cell_send[...] = total[:buckets].reshape(buckets, 1, cap)
        else:
            value_send[group] = total.reshape(buckets, 8, cap)

    def move(bucket, group):
        source, dest, out_sem, in_sem = (
            (cell_send, cell_recv, cell_out_sem, cell_in_sem) if group is None else
            (value_send.at[group], value_recv.at[group], value_out_sem.at[group], value_in_sem.at[group]))
        return pltpu.make_async_remote_copy(
            src_ref=source.at[bucket], dst_ref=dest.at[bucket], send_sem=out_sem.at[bucket],
            recv_sem=in_sem.at[bucket], device_id=peer(bucket), device_id_type=MESH)

    order = [0] + [q for d in range(1, n_ev // 2) for q in (d, n_ev - d)] + [n_ev // 2]

    def send(group):
        each([(q, s) for q in order for s in range(3) if 3 * q + s != 1], lambda q, s: move(3 * q + s, group).start())
        if group is None:
            cell_recv[1] = cell_send[1]
        else:
            value_recv[group, 1] = value_send[group, 1]

    def project(p):
        loads[5 + p].wait()
        return lax.dot_general(basis[...], kernels[0, p], (((1,), (0,)), ((), ())), preferred_element_type=F32)

    def sent(group):
        each([(q, s) for q in order for s in range(3) if 3 * q + s != 1], lambda q, s: move(3 * q + s, group).wait_send())

    loads[0].wait()
    loads[1].wait()
    projected = [project(0)]
    bucket(0)
    pl.semaphore_wait(barrier, n_ev - 1 + n_ev * ((sp > 0).astype(jnp.int32) + (sp < n_sp - 1).astype(jnp.int32)))
    send(0)
    loads[3].wait()
    bucket(None)
    send(None)
    loads[4].wait()

    ids_hi = row_ids(32 * 8, cap, 8)
    ids_lo = row_ids(256, cap, 1)

    def scatter(group):
        field[0, group] = jnp.zeros(field.shape[2:], F32)
        for q in order:
            highs, lows = [], []
            for s in range(3):
                b = 3 * q + s
                if b != 1:
                    when(has[2 - s], lambda b=b: move(b, group).wait_recv())
                    if group == 0:
                        when(has[2 - s], lambda b=b: move(b, None).wait_recv())
                cells = cell_recv[b].astype(jnp.int32)
                if group == 0:
                    wide = jnp.broadcast_to((cells & 255).astype(F32).astype(BF16), ids_lo.shape)
                    hot_lo[q, :, s * cap:(s + 1) * cap] = jnp.where(
                        ids_lo == wide, jnp.ones_like(wide), jnp.zeros_like(wide))
                line = (cells >> 8).astype(F32)
                high, low = split(value_recv[group, b])
                high = jnp.concatenate([high, high], axis=0)
                low = jnp.concatenate([low, low], axis=0)
                highs.append(spread(ids_hi, line, high))
                lows.append(spread(ids_hi, line, low))
            right = hot_lo[q]
            left = jnp.concatenate(highs + lows, axis=1)
            part = lax.dot_general(left, jnp.concatenate([right, right], axis=1), NT, preferred_element_type=F32)
            part = part.reshape(4, 4, 2, 8, 256)
            for z in range(2):
                field[0, group, :, :, :, z * 256:(z + 1) * 256] += part[:, :, z]

    faces = (
        (ev < n_ev - 1, ev > 0, (ev + 1, sp), lambda t, g: field.at[t, g, 3]),
        (ev > 0, ev < n_ev - 1, (ev - 1, sp), lambda t, g: field.at[t, g, 0]),
        (sp < n_sp - 1, sp > 0, (ev, sp + 1), lambda t, g: field.at[t, g, :, 3]),
        (sp > 0, sp < n_sp - 1, (ev, sp - 1), lambda t, g: field.at[t, g, :, 0]),
    )
    def face_copy(t, g, face):
        _, _, device, source = faces[face]
        return pltpu.make_async_remote_copy(
            src_ref=source(t, g), dst_ref=halo.at[t, face, g], send_sem=halo_out_sem.at[t, face, g],
            recv_sem=halo_in_sem.at[t, face, g], device_id=device, device_id_type=MESH)

    def send_faces(t, g, which=range(4)):
        for face in which:
            when(faces[face][0], lambda face=face: face_copy(t, g, face).start())

    def faces_sent(t, g):
        for face in range(4):
            when(faces[face][0], lambda face=face: face_copy(t, g, face).wait_send())

    lane = lax.broadcasted_iota(jnp.int32, (32, 512), 1)
    def step(t, g):
        for face in range(4):
            when(faces[face][1], lambda face=face: face_copy(t, g, face).wait_recv())
        for a in (0, 3, 1, 2):
            center = field[t, g, a]
            above = halo[t, 0, g] if a == 0 else field[t, g, a - 1]
            below = halo[t, 1, g] if a == 3 else field[t, g, a + 1]
            around = above + below
            around += jnp.concatenate([halo[t, 2, g, a][None], center[:3]], axis=0)
            around += jnp.concatenate([center[1:], halo[t, 3, g, a][None]], axis=0)
            flat = center.reshape(32, 512)
            left = jnp.where(lane == 0, 0.0, pltpu.roll(flat, 1, 1))
            right = jnp.where(lane == 511, 0.0, pltpu.roll(flat, 511, 1))
            around += (left + right).reshape(4, 8, 512)
            coeff = diffusivity[a].reshape(4, 1, 512)
            new = center + coeff * (around - 6.0 * center)
            if t < STEPS - 1:
                field[t + 1, g, a] = new
                if a in (0, 3):
                    send_faces(t + 1, g, (1 if a == 0 else 0,))
            else:
                for b2 in range(4):
                    for zt in range(4):
                        out[pl.ds(g * 512 + a * 16 + zt * 4 + b2, 8, stride=64), :] = new[b2, :, zt * 128:(zt + 1) * 128]
        if t < STEPS - 1:
            send_faces(t + 1, g, (2, 3))

    projected += [project(1), project(2)]
    bucket(1)
    bucket(2)
    sent(0)
    send(1)
    send(2)
    scatter(0)
    send_faces(0, 0)
    scatter(1)
    send_faces(0, 1)
    scatter(2)
    send_faces(0, 2)
    for group in (None, 1, 2):
        sent(group)
    for t in range(STEPS):
        for g in range(3):
            step(t, g)
            if t > 0:
                faces_sent(t - 1, g)

    for g in range(3):
        faces_sent(STEPS - 1, g)


def solution(mesh):
    n_ev, n_sp = mesh.shape["ev"], mesh.shape["sp"]

    def per_device(kernels, basis, crossing, owner, target, diffusivity):
        import functools
        buckets = 3 * n_ev
        cap = crossing.shape[1] * crossing.shape[2] // (2 * n_ev)
        arguments = [pltpu.with_memory_space_constraint(x, pltpu.HBM) for x in (kernels, basis, crossing, owner, target, diffusivity)]
        result = pl.pallas_call(
            functools.partial(kernel, n_ev, n_sp),
            out_shape=jax.ShapeDtypeStruct((1536, 128), F32),
            in_specs=[pl.BlockSpec(memory_space=pl.ANY)] * 6,
            out_specs=pl.BlockSpec(memory_space=pltpu.VMEM),
            scratch_shapes=[
                *[pltpu.VMEM(x.shape, x.dtype) for x in arguments],
                pltpu.SemaphoreType.DMA((9,)),
                pltpu.VMEM((3, buckets, 8, cap), F32),
                pltpu.VMEM((buckets, 1, cap), F32),
                pltpu.VMEM((3, buckets, 8, cap), F32),
                pltpu.VMEM((buckets, 1, cap), F32),
                pltpu.VMEM((STEPS, 3, 4, 4, 8, 512), F32),
                pltpu.VMEM((STEPS, 4, 3, 4, 8, 512), F32),
                pltpu.VMEM((n_ev, 256, 3 * cap), BF16),
                pltpu.SemaphoreType.DMA((3, buckets)),
                pltpu.SemaphoreType.DMA((buckets,)),
                pltpu.SemaphoreType.DMA((3, buckets)),
                pltpu.SemaphoreType.DMA((buckets,)),
                pltpu.SemaphoreType.DMA((STEPS, 4, 3)),
                pltpu.SemaphoreType.DMA((STEPS, 4, 3)),
            ],
            compiler_params=pltpu.CompilerParams(
                collective_id=0, has_side_effects=True, vmem_limit_bytes=40 * 1024 * 1024),
        )(*arguments)
        result = result.reshape(24, 4, 4, 4, 128).transpose(0, 1, 3, 2, 4)
        return result.reshape(24, 4, 4, 512)

    return jax.shard_map(
        per_device,
        mesh=mesh,
        in_specs=(
            P("ev", None, None, "sp"),
            P(),
            P("ev", None, "sp"),
            P("ev", None, "sp"),
            P("ev", None, "sp"),
            P("ev", "sp", None),
        ),
        out_specs=P(None, "ev", "sp", None),
        check_vma=False,
    )
```

```python
import jax
import jax.numpy as jnp
from jax import lax
from jax.experimental import pallas as pl
from jax.experimental.pallas import tpu as pltpu
from jax.sharding import PartitionSpec as P

MESH = pl.DeviceIdType.MESH
STEPS = 4
F32 = jnp.float32
BF16 = jnp.bfloat16
NT = (((1,), (1,)), ((), ()))


def split(value):
    high = value.astype(BF16)
    low = (value - high.astype(F32)).astype(BF16)
    return high, low


def row_ids(rows, columns, group):
    return (lax.broadcasted_iota(jnp.int32, (rows, columns), 0) // group).astype(F32).astype(BF16)


def spread(ids, row, values):
    repeats = ids.shape[0] // values.shape[0]
    wide = jnp.broadcast_to(row.astype(BF16), ids.shape)
    tiled = jnp.concatenate([values] * repeats, axis=0)
    return jnp.where(ids == wide, tiled, jnp.zeros_like(tiled))


def kernel(n_ev, n_sp, *refs):
    sources, out, inputs, input_sem = refs[:6], refs[6], refs[7:13], refs[13]
    loads = [pltpu.make_async_copy(sources[i], inputs[i], input_sem.at[i]) for i in range(1, 6)]
    loads += [pltpu.make_async_copy(sources[0].at[:, p], inputs[0].at[:, p], input_sem.at[6 + p]) for p in range(3)]
    for i in (2, 0, 5, 1, 6, 7, 3, 4):
        loads[i].start()
    body(n_ev, n_sp, loads, *inputs, out, *refs[14:])


def body(n_ev, n_sp, loads, kernels, basis, crossing, owner, target, diffusivity, out,
           value_send, cell_send, value_recv, cell_recv, field, halo, hot_lo,
           value_out_sem, cell_out_sem, value_in_sem, cell_in_sem, halo_out_sem, halo_in_sem):
    ev = lax.axis_index("ev")
    sp = lax.axis_index("sp")
    buckets = 3 * n_ev
    slots, elements = crossing.shape[1], crossing.shape[2]
    cap = value_send.shape[3]
    has = {0: sp > 0, 1: None, 2: sp < n_sp - 1}

    def when(condition, body):
        if condition is None:
            body()
        else:
            pl.when(condition)(body)

    inside = jnp.logical_and(sp > 0, sp < n_sp - 1)

    def each(pairs, act):
        @pl.when(inside)
        def _():
            for q, s in pairs:
                act(q, s)

        @pl.when(jnp.logical_not(inside))
        def _():
            for q, s in pairs:
                when(has[s], lambda q=q, s=s: act(q, s))

    def peer(bucket):
        return (lax.rem(ev + bucket // 3, n_ev), sp + bucket % 3 - 1)

    barrier = pltpu.get_barrier_semaphore()
    distant = [half for d in range(1, n_ev // 2) for half in (n_ev - d, d)]
    each([(q, s) for q in [n_ev // 2] + distant[::-1] + [0] for s in range(3) if 3 * q + s != 1], lambda q, s: pl.semaphore_signal(
        barrier, inc=1, device_id=peer(3 * q + s), device_id_type=MESH))

    for side, missing in ((2, sp == 0), (0, sp == n_sp - 1)):
        @pl.when(missing)
        def _(side=side):
            for q in range(n_ev):
                value_recv[:, 3 * q + side] = jnp.zeros((3,) + value_recv.shape[2:], F32)
                cell_recv[3 * q + side] = jnp.zeros(cell_recv.shape[1:], F32)
    for face, missing in enumerate((ev == 0, ev == n_ev - 1, sp == 0, sp == n_sp - 1)):
        @pl.when(missing)
        def _(face=face):
            for t in range(STEPS):
                halo[t, face] = jnp.zeros(halo.shape[2:], F32)

    loads[2].wait()
    owners = owner[0]
    row = lax.rem((owners >> 5) - ev + n_ev, n_ev)
    side = (owners & (n_sp - 1)) - sp + 1
    bucket_of = (row * 3 + side).astype(F32)
    chunk = 256
    per = elements // chunk
    ids32 = lax.broadcasted_iota(jnp.int32, (32, chunk), 0).astype(F32)
    hots = []
    for k in range(slots):
        for h in range(per):
            line = bucket_of[k:k + 1, h * chunk:(h + 1) * chunk]
            hots.append(jnp.where(ids32 == line, 1.0, 0.0))
    hot = jnp.concatenate(hots, axis=0).astype(BF16)
    ri = lax.broadcasted_iota(jnp.int32, (chunk, chunk), 0)
    ci = lax.broadcasted_iota(jnp.int32, (chunk, chunk), 1)
    before = jnp.where(ri < ci, 1.0, 0.0).astype(BF16)
    prefix = jnp.dot(hot, before, preferred_element_type=F32)
    total = jnp.dot(hot, jnp.ones((chunk, chunk), BF16), preferred_element_type=F32)
    carry = jnp.zeros((32, chunk), F32)
    rank_ids = row_ids(cap, chunk, 1)
    ranks = []
    for i in range(slots * per):
        rank = jnp.sum(hots[i] * (prefix[32 * i:32 * i + 32] + carry), axis=0, keepdims=True)
        carry = carry + total[32 * i:32 * i + 32]
        wide = jnp.broadcast_to(rank.astype(BF16), rank_ids.shape)
        ranks.append(jnp.where(rank_ids == wide, jnp.ones_like(wide), jnp.zeros_like(wide)))
    def bucket(group):
        total = None
        for k in range(slots):
            line = bucket_of[k:k + 1, :]
            hot_rank = jnp.concatenate(ranks[k * per:(k + 1) * per], axis=1)
            if group is None:
                cells = target[0, k:k + 1, :]
                high = jnp.broadcast_to((cells & -256).astype(F32).astype(BF16), (16, elements))
                low = jnp.broadcast_to((cells & 255).astype(F32).astype(BF16), (16, elements))
                ids = row_ids(32, elements, 1)
            else:
                high, low = split(projected[group] * crossing[0, k:k + 1, :])
                high = jnp.concatenate([high, high], axis=0)
                low = jnp.concatenate([low, low], axis=0)
                ids = row_ids(buckets * 8, elements, 8)
            left = jnp.concatenate([spread(ids, line, high), spread(ids, line, low)], axis=0)
            part = lax.dot_general(left, hot_rank, NT, preferred_element_type=F32)
            total = part if k == 0 else total + part
        total = total[:total.shape[0] // 2] + total[total.shape[0] // 2:]
        if group is None:
            cell_send[...] = total[:buckets].reshape(buckets, 1, cap)
        else:
            value_send[group] = total.reshape(buckets, 8, cap)

    def move(bucket, group):
        source, dest, out_sem, in_sem = (
            (cell_send, cell_recv, cell_out_sem, cell_in_sem) if group is None else
            (value_send.at[group], value_recv.at[group], value_out_sem.at[group], value_in_sem.at[group]))
        return pltpu.make_async_remote_copy(
            src_ref=source.at[bucket], dst_ref=dest.at[bucket], send_sem=out_sem.at[bucket],
            recv_sem=in_sem.at[bucket], device_id=peer(bucket), device_id_type=MESH)

    order = [0] + [q for d in range(1, n_ev // 2) for q in (d, n_ev - d)] + [n_ev // 2]

    def send(group):
        each([(q, s) for q in order for s in range(3) if 3 * q + s != 1], lambda q, s: move(3 * q + s, group).start())
        if group is None:
            cell_recv[1] = cell_send[1]
        else:
            value_recv[group, 1] = value_send[group, 1]

    def project(p):
        loads[5 + p].wait()
        return lax.dot_general(basis[...], kernels[0, p], (((1,), (0,)), ((), ())), preferred_element_type=F32)

    def sent(group, rows=order):
        each([(q, s) for q in rows for s in range(3) if 3 * q + s != 1], lambda q, s: move(3 * q + s, group).wait_send())

    loads[0].wait()
    loads[1].wait()
    projected = [project(0)]
    bucket(0)
    pl.semaphore_wait(barrier, n_ev - 1 + n_ev * ((sp > 0).astype(jnp.int32) + (sp < n_sp - 1).astype(jnp.int32)))
    send(0)
    loads[3].wait()
    bucket(None)
    send(None)
    loads[4].wait()

    ids_hi = row_ids(32 * 8, cap, 8)
    ids_lo = row_ids(256, cap, 1)

    def scatter(group):
        field[0, group] = jnp.zeros(field.shape[2:], F32)
        for q in order:
            highs, lows = [], []
            for s in range(3):
                b = 3 * q + s
                if b != 1:
                    when(has[2 - s], lambda b=b: move(b, group).wait_recv())
                    if group == 0:
                        when(has[2 - s], lambda b=b: move(b, None).wait_recv())
                cells = cell_recv[b].astype(jnp.int32)
                if group == 0:
                    wide = jnp.broadcast_to((cells & 255).astype(F32).astype(BF16), ids_lo.shape)
                    hot_lo[q, :, s * cap:(s + 1) * cap] = jnp.where(
                        ids_lo == wide, jnp.ones_like(wide), jnp.zeros_like(wide))
                line = (cells >> 8).astype(F32)
                high, low = split(value_recv[group, b])
                high = jnp.concatenate([high, high], axis=0)
                low = jnp.concatenate([low, low], axis=0)
                highs.append(spread(ids_hi, line, high))
                lows.append(spread(ids_hi, line, low))
            right = hot_lo[q]
            left = jnp.concatenate(highs + lows, axis=1)
            part = lax.dot_general(left, jnp.concatenate([right, right], axis=1), NT, preferred_element_type=F32)
            part = part.reshape(4, 4, 2, 8, 256)
            for z in range(2):
                field[0, group, :, :, :, z * 256:(z + 1) * 256] += part[:, :, z]

    faces = (
        (ev < n_ev - 1, ev > 0, (ev + 1, sp), lambda t, g: field.at[t, g, 3]),
        (ev > 0, ev < n_ev - 1, (ev - 1, sp), lambda t, g: field.at[t, g, 0]),
        (sp < n_sp - 1, sp > 0, (ev, sp + 1), lambda t, g: field.at[t, g, :, 3]),
        (sp > 0, sp < n_sp - 1, (ev, sp - 1), lambda t, g: field.at[t, g, :, 0]),
    )
    def face_copy(t, g, face):
        _, _, device, source = faces[face]
        return pltpu.make_async_remote_copy(
            src_ref=source(t, g), dst_ref=halo.at[t, face, g], send_sem=halo_out_sem.at[t, face, g],
            recv_sem=halo_in_sem.at[t, face, g], device_id=device, device_id_type=MESH)

    def send_faces(t, g, which=range(4)):
        for face in which:
            when(faces[face][0], lambda face=face: face_copy(t, g, face).start())

    def faces_sent(t, g):
        for face in range(4):
            when(faces[face][0], lambda face=face: face_copy(t, g, face).wait_send())

    lane = lax.broadcasted_iota(jnp.int32, (32, 512), 1)
    def step(t, g):
        for face in range(4):
            when(faces[face][1], lambda face=face: face_copy(t, g, face).wait_recv())
        for a in (0, 3, 1, 2):
            center = field[t, g, a]
            above = halo[t, 0, g] if a == 0 else field[t, g, a - 1]
            below = halo[t, 1, g] if a == 3 else field[t, g, a + 1]
            around = above + below
            around += jnp.concatenate([halo[t, 2, g, a][None], center[:3]], axis=0)
            around += jnp.concatenate([center[1:], halo[t, 3, g, a][None]], axis=0)
            flat = center.reshape(32, 512)
            left = jnp.where(lane == 0, 0.0, pltpu.roll(flat, 1, 1))
            right = jnp.where(lane == 511, 0.0, pltpu.roll(flat, 511, 1))
            around += (left + right).reshape(4, 8, 512)
            coeff = diffusivity[a].reshape(4, 1, 512)
            new = center + coeff * (around - 6.0 * center)
            if t < STEPS - 1:
                field[t + 1, g, a] = new
                if a in (0, 3):
                    send_faces(t + 1, g, (1 if a == 0 else 0,))
            else:
                for b2 in range(4):
                    for zt in range(4):
                        out[pl.ds(g * 512 + a * 16 + zt * 4 + b2, 8, stride=64), :] = new[b2, :, zt * 128:(zt + 1) * 128]
        if t < STEPS - 1:
            send_faces(t + 1, g, (2, 3))

    projected += [project(1), project(2)]
    bucket(1)
    bucket(2)
    sent(0, order[:5])
    send(1)
    send(2)
    scatter(0)
    send_faces(0, 0)
    scatter(1)
    send_faces(0, 1)
    scatter(2)
    send_faces(0, 2)
    sent(0, order[5:])
    for group in (None, 1, 2):
        sent(group)
    for t in range(STEPS):
        for g in range(3):
            step(t, g)
            if t > 0:
                faces_sent(t - 1, g)

    for g in range(3):
        faces_sent(STEPS - 1, g)


def solution(mesh):
    n_ev, n_sp = mesh.shape["ev"], mesh.shape["sp"]

    def per_device(kernels, basis, crossing, owner, target, diffusivity):
        import functools
        buckets = 3 * n_ev
        cap = crossing.shape[1] * crossing.shape[2] // (2 * n_ev)
        arguments = [pltpu.with_memory_space_constraint(x, pltpu.HBM) for x in (kernels, basis, crossing, owner, target, diffusivity)]
        result = pl.pallas_call(
            functools.partial(kernel, n_ev, n_sp),
            out_shape=jax.ShapeDtypeStruct((1536, 128), F32),
            in_specs=[pl.BlockSpec(memory_space=pl.ANY)] * 6,
            out_specs=pl.BlockSpec(memory_space=pltpu.VMEM),
            scratch_shapes=[
                *[pltpu.VMEM(x.shape, x.dtype) for x in arguments],
                pltpu.SemaphoreType.DMA((9,)),
                pltpu.VMEM((3, buckets, 8, cap), F32),
                pltpu.VMEM((buckets, 1, cap), F32),
                pltpu.VMEM((3, buckets, 8, cap), F32),
                pltpu.VMEM((buckets, 1, cap), F32),
                pltpu.VMEM((STEPS, 3, 4, 4, 8, 512), F32),
                pltpu.VMEM((STEPS, 4, 3, 4, 8, 512), F32),
                pltpu.VMEM((n_ev, 256, 3 * cap), BF16),
                pltpu.SemaphoreType.DMA((3, buckets)),
                pltpu.SemaphoreType.DMA((buckets,)),
                pltpu.SemaphoreType.DMA((3, buckets)),
                pltpu.SemaphoreType.DMA((buckets,)),
                pltpu.SemaphoreType.DMA((STEPS, 4, 3)),
                pltpu.SemaphoreType.DMA((STEPS, 4, 3)),
            ],
            compiler_params=pltpu.CompilerParams(
                collective_id=0, has_side_effects=True, vmem_limit_bytes=40 * 1024 * 1024),
        )(*arguments)
        result = result.reshape(24, 4, 4, 4, 128).transpose(0, 1, 3, 2, 4)
        return result.reshape(24, 4, 4, 512)

    return jax.shard_map(
        per_device,
        mesh=mesh,
        in_specs=(
            P("ev", None, None, "sp"),
            P(),
            P("ev", None, "sp"),
            P("ev", None, "sp"),
            P("ev", None, "sp"),
            P("ev", "sp", None),
        ),
        out_specs=P(None, "ev", "sp", None),
        check_vma=False,
    )
```
